256 devices in a mesh: store: 32 (over x, z), tensor: 8 (over y, core).
Axes of the slice: x: 4, y: 4, z: 8, core: 2. Of those that a mesh axis runs over, the one named last changes fastest.
Arguments:
- hidden: bfloat16 [32768, 12288], P('store', 'tensor'), may hold values from -6 to 6
- kv_weight: bfloat16 [12288, 2048], P('tensor', 'store'), may hold values from -0.0546875 to 0.0546875
- pages: bfloat16 [1024, 128, 2048], P('store', None, 'tensor'), may hold values from -8 to 8
- queries: bfloat16 [32768, 6144], P('store', 'tensor'), may hold values from -8 to 8
- page_owner: int32 [64, 16], replicated, may hold values from 0 to 31, as said below
- page_slot: int32 [64, 16], replicated, may hold values from 0 to 31
- span_order: int32 [64, 16], P('store'), may hold values from 0 to 15, each once within a row
- positions: int32 [64, 16, 32], P('store'), may hold values from 2 to 127, as said below
- counts: int32 [64, 16], P('store'), may hold values from 1 to 32, as said below
Outputs:
- attended: bfloat16 [32768, 6144], P('store', 'tensor')
- new_kv: bfloat16 [32768, 2048], P('store', 'tensor')
The draws below stay inside these ranges and needn't reach their ends.
Inputs may be any that keep to these rules, and one draw needn't show every extreme that they name: `page_owner`: request r is served at store index r // 2. Among the 32 pages of the requests served at one store index, each owner holds at most 2, and some owner exactly 2. `positions`: each row increases strictly. `counts`: every request has a span with 32.
All inputs are finite; a program needn't handle non-finite values.
Results may differ from the reference program's by a relative error of at most 0.0053.
Values may be sent and summed in bfloat16 or wider, within the bound.
No kernel may reach another device: no remote copies, remote signals or barrier semaphores. Data moves between devices by JAX's collectives and lax.ppermute only.
A program may use at most 128 MiB of HBM per device.

```python
import math
import jax
import jax.numpy as jnp
from jax import lax

D = 12288
HEAD = 128
KVH = 8
QH = 48
SPAN = 128
SPANS = 16
RB = 32
REQ_DEV = 2
REQUESTS = 64
CAP = 2
SLOTS = 32
ROWS = 32768
N_STORE = 32


def page_table(key):
    entries = REQ_DEV * SPANS
    capacity_all = N_STORE * CAP
    group_keys = jax.random.split(jax.random.fold_in(key, 21), N_STORE)

    def one_group(group_key):
        first_key, second_key = jax.random.split(group_key)
        shuffled = jax.random.permutation(first_key, capacity_all)
        chosen = shuffled[0] // CAP
        ranking = jnp.where(shuffled // CAP == chosen, shuffled % CAP, CAP + jnp.arange(capacity_all))
        picked = shuffled[jnp.argsort(ranking)][:entries] // CAP
        return jax.random.permutation(second_key, picked)
    owners = jax.vmap(one_group)(group_keys).reshape(REQUESTS, SPANS).astype(jnp.int32)
    slot_table = jax.random.randint(jax.random.fold_in(key, 22), (REQUESTS, SPANS), 0, SLOTS).astype(jnp.int32)
    return (owners, slot_table)


def draw_page_owner(key, part):
    return page_table(key)[0]


def draw_page_slot(key, part):
    return page_table(key)[1]


def draw_pages(key, part):
    key = jax.random.fold_in(key, 31)
    base = jnp.clip(jax.random.normal(key, (N_STORE * SLOTS, SPAN, KVH * 2 * HEAD), jnp.float32), -8.0, 8.0)
    return base.astype(jnp.bfloat16)


def draw_queries(key, part):
    key = jax.random.fold_in(key, 41)
    base = jnp.clip(jax.random.normal(key, (ROWS, QH * HEAD), jnp.float32), -8.0, 8.0)
    return base.astype(jnp.bfloat16)


def draw_positions(key, part):
    key = jax.random.fold_in(key, 51)
    row_keys = jax.random.split(key, REQUESTS * SPANS)

    def one_row(row_key):
        return jnp.sort(jax.random.permutation(row_key, SPAN - 2)[:RB]) + 2
    return jax.vmap(one_row)(row_keys).reshape(REQUESTS, SPANS, RB).astype(jnp.int32)


def draw_counts(key, part):
    key = jax.random.fold_in(key, 61)
    drawn = jax.random.randint(jax.random.fold_in(key, 1), (REQUESTS, SPANS), 1, RB + 1)
    full_at = jax.random.randint(jax.random.fold_in(key, 2), (REQUESTS, 1), 0, SPANS)
    return jnp.where(jnp.arange(SPANS)[None, :] == full_at, RB, drawn).astype(jnp.int32)


def block_scale(own_key, shape, cuts, low, high):
    gain = 1.0
    for dim, parts in cuts:
        heights = jax.random.uniform(jax.random.fold_in(jax.random.fold_in(own_key, 6), dim), (parts,), jnp.float32, low / len(cuts), high / len(cuts))
        gain = gain * jnp.repeat(jnp.exp(heights), shape[dim] // parts).reshape((-1,) + (1,) * (len(shape) - 1 - dim))
    return gain


def scatter_about(rng, dims, spread, bound, shards=(), kind=jnp.bfloat16):
    level = block_scale(rng, dims, shards, -0.22, 0.18) if shards else 1.0
    values = jax.random.normal(rng, dims, jnp.float32) * spread * level
    return jnp.minimum(jnp.maximum(values, -bound), bound).astype(kind)


def setup_inputs(seed: int = 0) -> dict:
    keys = jax.random.split(jax.random.key(seed), 10)
    return {
        "hidden": scatter_about(keys[0], (ROWS, D), 1.0, 6.0, ((0, 32), (1, 8))),
        "kv_weight": scatter_about(keys[1], (D, KVH * 2 * HEAD), D ** -0.5, 0.0546875, ((0, 8), (1, 32))),
        "pages": draw_pages(jax.random.fold_in(keys[9], 71), 0),
        "queries": draw_queries(jax.random.fold_in(keys[9], 71), 0),
        "page_owner": draw_page_owner(jax.random.fold_in(keys[9], 71), 0),
        "page_slot": draw_page_slot(jax.random.fold_in(keys[9], 71), 0),
        "span_order": jax.vmap(lambda own: jax.random.permutation(own, SPANS))(jax.random.split(keys[6], REQUESTS)).reshape((REQUESTS, SPANS)).astype(jnp.int32),
        "positions": draw_positions(jax.random.fold_in(keys[9], 71), 0),
        "counts": draw_counts(jax.random.fold_in(keys[9], 71), 0),
    }


def blend_attend(request_queries, fresh_rows, cached, span_rank, recompute_pos, row_used):
    spans, span_len, kv_width = cached.shape
    per_span = recompute_pos.shape[1]
    kv_heads = kv_width // (2 * HEAD)
    head_group = request_queries.shape[1] // (kv_heads * HEAD)
    marked = (recompute_pos[:, :, None] == jnp.arange(span_len)[None, None, :]) & row_used[:, :, None]
    placed = jnp.einsum('cjt,cjw->ctw', marked.astype(jnp.float32), fresh_rows.reshape(spans, per_span, kv_width).astype(jnp.float32))
    replaced = jnp.any(marked, axis=1)[:, :, None]
    blended = jnp.where(replaced, placed, cached.astype(jnp.float32)).astype(jnp.bfloat16)
    key_value = blended.reshape(spans * span_len, kv_heads, 2, HEAD).astype(jnp.float32)
    query_rows = request_queries.reshape(spans * per_span, kv_heads, head_group, HEAD).astype(jnp.float32)
    scores = jnp.einsum('qhgd,khd->hgqk', query_rows, key_value[:, :, 0]) * (1.0 / math.sqrt(HEAD))
    query_span = jnp.arange(spans * per_span) // per_span
    key_span = jnp.arange(spans * span_len) // span_len
    key_place = jnp.arange(spans * span_len) % span_len
    query_place = recompute_pos.reshape(-1)
    query_rank = jnp.repeat(span_rank, per_span)
    key_rank = jnp.repeat(span_rank, span_len)
    earlier = key_rank[None, :] < query_rank[:, None]
    causal = (key_span[None, :] == query_span[:, None]) & (key_place[None, :] <= query_place[:, None])
    allowed = earlier | causal
    scores = jnp.where(allowed[None, None], scores, -1e+30)
    peak = lax.optimization_barrier(jnp.max(scores, axis=-1, keepdims=True))
    raised = jnp.exp(scores - peak)
    weights = (raised / lax.optimization_barrier(jnp.sum(raised, axis=-1, keepdims=True))).astype(jnp.bfloat16)
    mixed = jnp.einsum('hgqk,khd->qhgd', weights.astype(jnp.float32), key_value[:, :, 1])
    mixed = mixed.reshape(spans * per_span, -1) * row_used.reshape(-1, 1).astype(jnp.float32)
    return mixed.astype(jnp.bfloat16)

def reference(hidden, kv_weight, pages, queries, page_owner, page_slot, span_order, positions, counts):
    rows_request = SPANS * RB
    hidden_request = hidden.reshape(REQUESTS, rows_request, D)
    query_request = queries.reshape(REQUESTS, rows_request, QH * HEAD)
    page_index = (page_owner * SLOTS + page_slot).astype(jnp.int32)

    def one_request(inputs):
        hidden_rows, query_rows, index_row, rank_row, position_rows, count_row = inputs
        row_used = jnp.arange(RB)[None, :] < count_row[:, None]
        fresh_rows = jnp.dot(hidden_rows, kv_weight, preferred_element_type=jnp.float32)
        fresh_rows = (fresh_rows * row_used.reshape(-1, 1).astype(jnp.float32)).astype(jnp.bfloat16)
        cached = jnp.take(pages, index_row, axis=0)
        mixed = blend_attend(query_rows, fresh_rows, cached, rank_row, position_rows, row_used)
        return (mixed, fresh_rows)
    attended, new_kv = lax.map(one_request, (hidden_request, query_request, page_index, span_order, positions, counts))
    return (attended.reshape(ROWS, QH * HEAD), new_kv.reshape(ROWS, KVH * 2 * HEAD))
```

```python
import functools

import jax
import jax.numpy as jnp
from jax import lax
from jax.experimental import pallas as pl
from jax.experimental.pallas import tpu as pltpu
from jax.sharding import Mesh
from jax.sharding import PartitionSpec as P

HEAD = 128
BF16 = jnp.bfloat16
F32 = jnp.float32
STORE = ("x", "z")
TENSOR = ("y", "core")
NEG = -1e30
EXP2_SCALE = 1.4426950408889634 * HEAD**-0.5


def pack_kernel(slot_ref, pages_ref, out_ref, sems):
    count = out_ref.shape[0]

    def copy(i):
        return pltpu.make_async_copy(pages_ref.at[slot_ref[i]], out_ref.at[i], sems.at[i])

    def start(i, carry):
        copy(i).start()
        return carry

    def wait(i, carry):
        copy(i).wait()
        return carry

    lax.fori_loop(0, count, start, 0)
    lax.fori_loop(0, count, wait, 0)


def pack_pages(source_slot, pages):
    count = source_slot.shape[0]
    return pl.pallas_call(
        pack_kernel,
        out_shape=jax.ShapeDtypeStruct((count,) + pages.shape[1:], pages.dtype),
        in_specs=[
            pl.BlockSpec(memory_space=pltpu.SMEM),
            pl.BlockSpec(memory_space=pl.ANY),
        ],
        out_specs=pl.BlockSpec(memory_space=pl.ANY),
        scratch_shapes=[pltpu.SemaphoreType.DMA((count,))],
        cost_estimate=pl.CostEstimate(
            flops=0, bytes_accessed=4 * count * pages.shape[1] * pages.shape[2], transcendentals=0
        ),
    )(source_slot, pages)


def project_kernel(hidden_ref, weight_ref, out_ref):
    out_ref[0] = lax.dot_general(
        hidden_ref[...], weight_ref[...], (((1,), (1,)), ((), ())), preferred_element_type=F32
    ).astype(out_ref.dtype)


def project(hidden, weight_t, block):
    rows, width = hidden.shape
    columns = weight_t.shape[0]
    return pl.pallas_call(
        project_kernel,
        grid=(columns // block,),
        out_shape=jax.ShapeDtypeStruct((columns // block, rows, block), BF16),
        in_specs=[
            pl.BlockSpec((rows, width), lambda i: (0, 0)),
            pl.BlockSpec((block, width), lambda i: (i, 0)),
        ],
        out_specs=pl.BlockSpec((1, rows, block), lambda i: (i, 0, 0)),
        compiler_params=pltpu.CompilerParams(vmem_limit_bytes=40 << 20),
        cost_estimate=pl.CostEstimate(
            flops=2 * rows * width * columns,
            bytes_accessed=2 * (rows * width + columns * width + rows * columns),
            transcendentals=0,
        ),
    )(hidden, weight_t)


def attend_kernel(
    spans,
    per_span,
    page_ref,
    span_ref,
    count_ref,
    q_ref,
    new_ref,
    pos_row_ref,
    pos_lane_ref,
    arrived_ref,
    out_ref,
    raw,
    keys,
    values,
    scores,
    weights,
    sems,
):
    requests = raw.shape[0]
    span_len = arrived_ref.shape[1]
    heads = q_ref.shape[1] // HEAD
    half = heads * per_span
    rows_request = spans * per_span

    def copy(r, k):
        return pltpu.make_async_copy(
            arrived_ref.at[page_ref[r, k]],
            raw.at[r, pl.ds(k * span_len, span_len)],
            sems.at[r, k],
        )

    for r in range(requests):
        for k in range(spans):
            copy(r, k).start()
    values[:, :, HEAD:] = jnp.ones((requests, spans * span_len, HEAD), BF16)
    place = lax.broadcasted_iota(jnp.int32, (span_len, per_span), 0)
    slot = lax.broadcasted_iota(jnp.int32, (span_len, per_span), 1)
    lane = lax.broadcasted_iota(jnp.int32, (per_span, span_len), 1)
    sub = lax.broadcasted_iota(jnp.int32, (per_span, HEAD), 0)
    groups = [(r, g) for r in range(requests) for g in range(spans // 2)]

    def blend(r, k):
        c = span_ref[r, k]
        copy(r, k).wait()
        pos = pos_row_ref[pl.ds(r * spans + c, 1), :]
        marked = (place == pos) & (slot < count_ref[r, c])
        first = pl.multiple_of(r * rows_request + c * per_span, per_span)
        fresh = new_ref[pl.ds(first, per_span), :]
        placed = jnp.dot(marked.astype(F32).astype(BF16), fresh, preferred_element_type=F32)
        replaced = jnp.max(marked.astype(F32), axis=1, keepdims=True) > 0.5
        at = slice(k * span_len, (k + 1) * span_len)
        mixed = jnp.where(replaced, placed, raw[r, at, :].astype(F32)).astype(BF16)
        keys[r, at, :] = mixed[:, :HEAD]
        values[r, at, :HEAD] = mixed[:, HEAD:]

    def first_row(r, k):
        return pl.multiple_of(r * rows_request + span_ref[r, k] * per_span, per_span)

    def score(step):
        r, g = groups[step]
        length = (g + 1) * 2 * span_len
        stacked = []
        for k in (2 * g, 2 * g + 1):
            blend(r, k)
            block = q_ref[pl.ds(first_row(r, k), per_span), :]
            stacked += [block[:, h * HEAD : (h + 1) * HEAD] for h in range(heads)]
        scores[step % 2, :, :length] = lax.dot_general(
            jnp.concatenate(stacked, axis=0),
            keys[r, :length, :],
            (((1,), (1,)), ((), ())),
            preferred_element_type=F32,
        )

    def attend(step):
        r, g = groups[step]
        slot_now = step % 2
        length = (g + 1) * 2 * span_len
        for part, k in enumerate((2 * g, 2 * g + 1)):
            rows = slice(part * half, (part + 1) * half)
            own = k * span_len
            allowed = lane <= pos_lane_ref[pl.ds(first_row(r, k), per_span), :]
            allowed = jnp.concatenate([allowed] * heads, axis=0)
            diagonal = jnp.where(allowed, scores[slot_now, rows, own : own + span_len], NEG)
            peak = jnp.max(diagonal, axis=1, keepdims=True)
            if k:
                before = scores[slot_now, rows, :own]
                peak = jnp.maximum(peak, jnp.max(before, axis=1, keepdims=True))
                weights[slot_now, rows, :own] = jnp.exp2((before - peak) * EXP2_SCALE).astype(BF16)
            weights[slot_now, rows, own : own + span_len] = jnp.exp2(
                (diagonal - peak) * EXP2_SCALE
            ).astype(BF16)
            if own + span_len < length:
                weights[slot_now, rows, own + span_len : length] = jnp.zeros(
                    (half, length - own - span_len), BF16
                )
        mixed = jnp.dot(
            weights[slot_now, :, :length], values[r, :length, :], preferred_element_type=F32
        )
        mixed = mixed[:, :HEAD] / mixed[:, HEAD:]
        for part, k in enumerate((2 * g, 2 * g + 1)):
            used = sub < count_ref[r, span_ref[r, k]]
            for h in range(heads):
                at = part * half + h * per_span
                out_ref[pl.ds(first_row(r, k), per_span), h * HEAD : (h + 1) * HEAD] = jnp.where(
                    used, mixed[at : at + per_span], 0.0
                ).astype(BF16)

    score(0)
    for step in range(len(groups)):
        if step + 1 < len(groups):
            score(step + 1)
        attend(step)


def attend(page_at, span_at, counts, queries, new_kv, positions, arrived):
    requests, spans = span_at.shape
    per_span = positions.shape[2]
    span_len = arrived.shape[1]
    kv_width = arrived.shape[2]
    heads = queries.shape[1] // HEAD
    length = spans * span_len
    pos_row = positions.reshape(requests * spans, per_span)
    pos_lane = jnp.broadcast_to(
        positions.reshape(requests * spans * per_span, 1), (requests * spans * per_span, span_len)
    )
    smem = pl.BlockSpec(memory_space=pltpu.SMEM)
    vmem = pl.BlockSpec(memory_space=pltpu.VMEM)
    pair = 2 * heads * per_span
    return pl.pallas_call(
        functools.partial(attend_kernel, spans, per_span),
        out_shape=jax.ShapeDtypeStruct(queries.shape, BF16),
        in_specs=[smem, smem, smem, vmem, vmem, vmem, vmem, pl.BlockSpec(memory_space=pl.ANY)],
        out_specs=vmem,
        scratch_shapes=[
            pltpu.VMEM((requests, length, kv_width), BF16),
            pltpu.VMEM((requests, length, HEAD), BF16),
            pltpu.VMEM((requests, length, 2 * HEAD), BF16),
            pltpu.VMEM((2, pair, length), F32),
            pltpu.VMEM((2, pair, length), BF16),
            pltpu.SemaphoreType.DMA((requests, spans)),
        ],
        compiler_params=pltpu.CompilerParams(vmem_limit_bytes=48 << 20),
        cost_estimate=pl.CostEstimate(
            flops=2 * requests * pair * length * HEAD * 3 * spans // 4,
            bytes_accessed=4 * queries.size + 2 * arrived.size,
            transcendentals=requests * pair * length * spans // 4,
        ),
    )(page_at, span_at, counts, queries, new_kv, pos_row, pos_lane, arrived)


def gather_weight(weight_t):
    return lax.all_gather(weight_t, STORE, axis=0, tiled=True)


def body(hidden, kv_weight, pages, queries, page_owner, page_slot, span_order, positions, counts):
    stores = lax.axis_size(STORE)
    tensors = lax.axis_size(TENSOR)
    store_index = lax.axis_index(STORE)
    requests, spans = span_order.shape
    per_span = positions.shape[2]
    entries = requests * spans
    span_len, kv_width = pages.shape[1:]

    owners = page_owner.reshape(stores, entries)
    slots = page_slot.reshape(stores, entries)
    entry = jnp.arange(entries)[None, :]
    mine = owners == store_index
    code = entry * pages.shape[0] + slots
    first = jnp.min(jnp.where(mine, code, entries * pages.shape[0]), axis=1)
    last = jnp.max(jnp.where(mine, code, 0), axis=1)
    source_slot = jnp.stack([first, last], axis=1).reshape(-1) % pages.shape[0]
    outgoing = pack_pages(source_slot, pages).reshape(stores, 2, span_len, kv_width)
    arrived = lax.all_to_all(outgoing, STORE, split_axis=0, concat_axis=0, tiled=True)
    arrived = arrived.reshape(stores * 2, span_len, kv_width)

    weight_t = gather_weight(kv_weight.T)
    partial_kv = project(hidden, weight_t, kv_width)
    own_kv = lax.psum_scatter(partial_kv, TENSOR, scatter_dimension=0, tiled=True)
    own_kv = own_kv.reshape(entries * per_span, kv_width)
    row_used = jnp.arange(per_span)[None, None, :] < counts[:, :, None]
    new_kv = jnp.where(row_used.reshape(-1, 1), own_kv, jnp.zeros((), BF16))

    my_owner = lax.dynamic_index_in_dim(owners, store_index, 0, keepdims=False)
    earlier = jnp.arange(entries)[None, :] < jnp.arange(entries)[:, None]
    second = jnp.any((my_owner[:, None] == my_owner[None, :]) & earlier, axis=1)
    page_of = (my_owner * 2 + second.astype(jnp.int32)).reshape(requests, spans)
    at_rank = span_order[:, None, :] == jnp.arange(spans)[None, :, None]
    span_at = jnp.sum(at_rank * jnp.arange(spans)[None, None, :], axis=2)
    page_at = jnp.sum(at_rank * page_of[:, None, :], axis=2)
    attended = attend(page_at, span_at, counts, queries, new_kv, positions, arrived)
    return attended, new_kv


def solution(mesh):
    split = Mesh(mesh.devices.reshape(4, 8, 4, 2), STORE + TENSOR)
    return jax.shard_map(
        body,
        mesh=split,
        in_specs=(
            P(STORE, TENSOR),
            P(TENSOR, STORE),
            P(STORE, None, TENSOR),
            P(STORE, TENSOR),
            P(),
            P(),
            P(STORE, None),
            P(STORE, None, None),
            P(STORE, None),
        ),
        out_specs=(P(STORE, TENSOR), P(STORE, TENSOR)),
        check_vma=False,
    )
```

```python
import functools

import jax
import jax.numpy as jnp
from jax import lax
from jax.experimental import pallas as pl
from jax.experimental.pallas import tpu as pltpu
from jax.sharding import Mesh
from jax.sharding import PartitionSpec as P

HEAD = 128
BF16 = jnp.bfloat16
F32 = jnp.float32
STORE = ("x", "z")
TENSOR = ("y", "core")
NEG = -1e30
EXP2_SCALE = 1.4426950408889634 * HEAD**-0.5


def pack_kernel(slot_ref, pages_ref, out_ref, sems):
    count = out_ref.shape[0]

    def copy(i):
        return pltpu.make_async_copy(pages_ref.at[slot_ref[i]], out_ref.at[i], sems.at[i])

    def start(i, carry):
        copy(i).start()
        return carry

    def wait(i, carry):
        copy(i).wait()
        return carry

    lax.fori_loop(0, count, start, 0)
    lax.fori_loop(0, count, wait, 0)


def pack_pages(source_slot, pages):
    count = source_slot.shape[0]
    return pl.pallas_call(
        pack_kernel,
        out_shape=jax.ShapeDtypeStruct((count,) + pages.shape[1:], pages.dtype),
        in_specs=[
            pl.BlockSpec(memory_space=pltpu.SMEM),
            pl.BlockSpec(memory_space=pl.ANY),
        ],
        out_specs=pl.BlockSpec(memory_space=pltpu.VMEM),
        scratch_shapes=[pltpu.SemaphoreType.DMA((count,))],
        cost_estimate=pl.CostEstimate(flops=0, bytes_accessed=1024, transcendentals=0),
    )(source_slot, pages)


def project_kernel(slot_ref, own_ref, other_ref, *rest):
    weights = rest[:4]
    outs = rest[4:8]
    held, sems = rest[8:]
    halves, slices, columns, width = weights[0].shape
    block = halves * columns
    copies = []
    for i in range(4):
        for j in range(halves):
            for s in range(slices):
                at = pl.multiple_of(slot_ref[i] * block + j * columns, columns)
                copies.append(
                    pltpu.make_async_copy(
                        weights[i].at[j, s], held.at[s, pl.ds(at, columns)], sems.at[i, j, s]
                    )
                )
    for copy in copies:
        copy.start()
    for copy in copies:
        copy.wait()
    step = 256
    for row in range(0, own_ref.shape[0], step):
        rows = slice(row, row + step)
        product = sum(
            lax.dot_general(
                ref[rows, :], held[s], (((1,), (1,)), ((), ())), preferred_element_type=F32
            )
            for s, ref in enumerate((own_ref, other_ref))
        )
        for i in range(4):
            outs[i][rows, :] = product[:, i * block : (i + 1) * block].astype(BF16)


def project(slots, own, other, weights):
    rows, width = own.shape
    halves, slices, columns, _ = weights[0].shape
    block = halves * columns
    vmem = pl.BlockSpec(memory_space=pltpu.VMEM)
    in_specs = [pl.BlockSpec(memory_space=pltpu.SMEM), vmem, vmem]
    in_specs += [pl.BlockSpec(memory_space=pl.ANY)] * 4
    return pl.pallas_call(
        project_kernel,
        out_shape=[jax.ShapeDtypeStruct((rows, block), BF16)] * 4,
        in_specs=in_specs,
        out_specs=[vmem] * 4,
        scratch_shapes=[
            pltpu.VMEM((slices, 4 * block, width), BF16),
            pltpu.SemaphoreType.DMA((4, halves, slices)),
        ],
        compiler_params=pltpu.CompilerParams(vmem_limit_bytes=40 << 20),
        cost_estimate=pl.CostEstimate(flops=0, bytes_accessed=1024, transcendentals=0),
    )(slots, own, other, *weights)


def attend_kernel(
    spans,
    per_span,
    page_ref,
    span_ref,
    count_ref,
    q_ref,
    new_ref,
    pos_row_ref,
    pos_lane_ref,
    arrived_ref,
    out_ref,
    raw,
    keys,
    values,
    scores,
    weights,
    sems,
):
    requests = raw.shape[0]
    span_len = arrived_ref.shape[1]
    heads = q_ref.shape[1] // HEAD
    half = heads * per_span
    rows_request = spans * per_span

    def copy(r, k):
        return pltpu.make_async_copy(
            arrived_ref.at[page_ref[r, k]],
            raw.at[r, pl.ds(k * span_len, span_len)],
            sems.at[r, k],
        )

    for r in range(requests):
        for k in range(spans):
            copy(r, k).start()
    values[:, :, HEAD:] = jnp.ones((requests, spans * span_len, HEAD), BF16)
    place = lax.broadcasted_iota(jnp.int32, (span_len, per_span), 0)
    slot = lax.broadcasted_iota(jnp.int32, (span_len, per_span), 1)
    lane = lax.broadcasted_iota(jnp.int32, (per_span, span_len), 1)
    sub = lax.broadcasted_iota(jnp.int32, (per_span, HEAD), 0)
    groups = [(r, g) for r in range(requests) for g in range(spans // 2)]

    def blend(r, k):
        c = span_ref[r, k]
        copy(r, k).wait()
        pos = pos_row_ref[pl.ds(r * spans + c, 1), :]
        marked = (place == pos) & (slot < count_ref[r, c])
        first = pl.multiple_of(r * rows_request + c * per_span, per_span)
        fresh = new_ref[pl.ds(first, per_span), :]
        placed = jnp.dot(marked.astype(F32).astype(BF16), fresh, preferred_element_type=F32)
        replaced = jnp.max(marked.astype(F32), axis=1, keepdims=True) > 0.5
        at = slice(k * span_len, (k + 1) * span_len)
        mixed = jnp.where(replaced, placed, raw[r, at, :].astype(F32)).astype(BF16)
        keys[r, at, :] = mixed[:, :HEAD]
        values[r, at, :HEAD] = mixed[:, HEAD:]

    def first_row(r, k):
        return pl.multiple_of(r * rows_request + span_ref[r, k] * per_span, per_span)

    def score(step):
        r, g = groups[step]
        length = (g + 1) * 2 * span_len
        stacked = []
        for k in (2 * g, 2 * g + 1):
            blend(r, k)
            block = q_ref[pl.ds(first_row(r, k), per_span), :]
            stacked += [block[:, h * HEAD : (h + 1) * HEAD] for h in range(heads)]
        scores[step % 2, :, :length] = lax.dot_general(
            jnp.concatenate(stacked, axis=0),
            keys[r, :length, :],
            (((1,), (1,)), ((), ())),
            preferred_element_type=F32,
        )

    def attend(step):
        r, g = groups[step]
        slot_now = step % 2
        length = (g + 1) * 2 * span_len
        for part, k in enumerate((2 * g, 2 * g + 1)):
            rows = slice(part * half, (part + 1) * half)
            own = k * span_len
            allowed = lane <= pos_lane_ref[pl.ds(first_row(r, k), per_span), :]
            allowed = jnp.concatenate([allowed] * heads, axis=0)
            diagonal = jnp.where(allowed, scores[slot_now, rows, own : own + span_len], NEG)
            peak = jnp.max(diagonal, axis=1, keepdims=True)
            if k:
                before = scores[slot_now, rows, :own]
                peak = jnp.maximum(peak, jnp.max(before, axis=1, keepdims=True))
                weights[slot_now, rows, :own] = jnp.exp2((before - peak) * EXP2_SCALE).astype(BF16)
            weights[slot_now, rows, own : own + span_len] = jnp.exp2(
                (diagonal - peak) * EXP2_SCALE
            ).astype(BF16)
            if own + span_len < length:
                weights[slot_now, rows, own + span_len : length] = jnp.zeros(
                    (half, length - own - span_len), BF16
                )
        mixed = jnp.dot(
            weights[slot_now, :, :length], values[r, :length, :], preferred_element_type=F32
        )
        mixed = mixed[:, :HEAD] / mixed[:, HEAD:]
        for part, k in enumerate((2 * g, 2 * g + 1)):
            used = sub < count_ref[r, span_ref[r, k]]
            for h in range(heads):
                at = part * half + h * per_span
                out_ref[pl.ds(first_row(r, k), per_span), h * HEAD : (h + 1) * HEAD] = jnp.where(
                    used, mixed[at : at + per_span], 0.0
                ).astype(BF16)

    score(0)
    for step in range(len(groups)):
        if step + 1 < len(groups):
            score(step + 1)
        attend(step)


def attend(page_at, span_at, counts, queries, new_kv, positions, arrived):
    requests, spans = span_at.shape
    per_span = positions.shape[2]
    span_len = arrived.shape[1]
    kv_width = arrived.shape[2]
    heads = queries.shape[1] // HEAD
    length = spans * span_len
    pos_row = positions.reshape(requests * spans, per_span)
    pos_lane = jnp.broadcast_to(
        positions.reshape(requests * spans * per_span, 1), (requests * spans * per_span, span_len)
    )
    smem = pl.BlockSpec(memory_space=pltpu.SMEM)
    vmem = pl.BlockSpec(memory_space=pltpu.VMEM)
    pair = 2 * heads * per_span
    return pl.pallas_call(
        functools.partial(attend_kernel, spans, per_span),
        out_shape=jax.ShapeDtypeStruct(queries.shape, BF16),
        in_specs=[smem, smem, smem, vmem, vmem, vmem, vmem, pl.BlockSpec(memory_space=pl.ANY)],
        out_specs=vmem,
        scratch_shapes=[
            pltpu.VMEM((requests, length, kv_width), BF16),
            pltpu.VMEM((requests, length, HEAD), BF16),
            pltpu.VMEM((requests, length, 2 * HEAD), BF16),
            pltpu.VMEM((2, pair, length), F32),
            pltpu.VMEM((2, pair, length), BF16),
            pltpu.SemaphoreType.DMA((requests, spans)),
        ],
        compiler_params=pltpu.CompilerParams(vmem_limit_bytes=48 << 20),
        cost_estimate=pl.CostEstimate(flops=0, bytes_accessed=1024, transcendentals=0),
    )(page_at, span_at, counts, queries, new_kv, pos_row, pos_lane, arrived)


def shift(x, axis, by):
    size = lax.axis_size(axis)
    return lax.ppermute(x, axis, [(i, (i + by) % size) for i in range(size)])


def gather_over_z(pair):
    z = lax.axis_index("z")
    core = lax.axis_index("core")
    gathered = jnp.zeros((4,) + pair.shape, BF16)
    for by in range(4):
        near = []
        for hop in (by, by + 4):
            moves = [(s * 2 + s // 4, (s + hop) % 8 * 2 + s // 4) for s in range(8)]
            near.append(lax.ppermute(pair, ("z", "core"), moves) if hop else pair)
        first = (z - by) % 8 // 4 == core
        piece = jnp.where(first, near[0], near[1])
        gathered = lax.dynamic_update_slice(gathered, piece[None], ((z - by) % 4, 0, 0, 0))
    return gathered


def new_rows(hidden, gathered):
    ahead = (lax.axis_index("x") - lax.axis_index("y") - jnp.arange(4)) % 4
    other = shift(hidden, "core", 1)
    parts = []
    for part in range(2):
        piece = gathered[2 * part : 2 * part + 2]
        parts.append([piece] + [shift(piece, "x", by) for by in (1, 2, 3)])
    totals = []
    for weights in parts:
        if totals:
            weights[0], products = lax.optimization_barrier((weights[0], products))
            received = [shift(products[by], "y", by) for by in (1, 3, 2)]
            totals[0] = sum((p.astype(F32) for p in received), products[0].astype(F32))
        products = project(ahead, hidden, other, weights)
        if not totals:
            totals.append(None)
        else:
            received = [shift(products[by], "y", by) for by in (1, 3, 2)]
            totals.append(sum((p.astype(F32) for p in received), products[0].astype(F32)))
    return jnp.concatenate(totals, axis=1)


def body(hidden, kv_weight, pages, queries, page_owner, page_slot, span_order, positions, counts):
    stores = lax.axis_size(STORE)
    tensors = lax.axis_size(TENSOR)
    store_index = lax.axis_index(STORE)
    requests, spans = span_order.shape
    per_span = positions.shape[2]
    entries = requests * spans
    span_len, kv_width = pages.shape[1:]

    owners = page_owner.reshape(stores, entries)
    slots = page_slot.reshape(stores, entries)
    entry = jnp.arange(entries)[None, :]
    mine = owners == store_index
    code = entry * pages.shape[0] + slots
    first = jnp.min(jnp.where(mine, code, entries * pages.shape[0]), axis=1)
    last = jnp.max(jnp.where(mine, code, 0), axis=1)
    source_slot = jnp.stack([first, last], axis=1).reshape(-1) % pages.shape[0]
    outgoing = pack_pages(source_slot, pages)
    shard, outgoing = lax.optimization_barrier((kv_weight.T, outgoing))
    pair = jnp.stack([shard, shift(shard, "core", 1)])
    gathered = gather_over_z(pair)
    outgoing = outgoing.reshape(4, 8, 2, span_len, kv_width)
    halfway = lax.all_to_all(outgoing, "x", split_axis=0, concat_axis=0, tiled=True)
    halfway = halfway.transpose(1, 0, 2, 3, 4)
    halfway, gathered = lax.optimization_barrier((halfway, gathered))
    arrived = lax.all_to_all(halfway, "z", split_axis=0, concat_axis=0, tiled=True)
    arrived = arrived.reshape(stores * 2, span_len, kv_width)

    own_kv = new_rows(hidden, gathered)
    row_used = jnp.arange(per_span)[None, None, :] < counts[:, :, None]
    new_kv = jnp.where(row_used.reshape(-1, 1), own_kv, 0.0).astype(BF16)

    my_owner = lax.dynamic_index_in_dim(owners, store_index, 0, keepdims=False)
    earlier = jnp.arange(entries)[None, :] < jnp.arange(entries)[:, None]
    second = jnp.any((my_owner[:, None] == my_owner[None, :]) & earlier, axis=1)
    page_of = ((my_owner % 8 * 4 + my_owner // 8) * 2 + second.astype(jnp.int32)).reshape(requests, spans)
    at_rank = span_order[:, None, :] == jnp.arange(spans)[None, :, None]
    span_at = jnp.sum(at_rank * jnp.arange(spans)[None, None, :], axis=2)
    page_at = jnp.sum(at_rank * page_of[:, None, :], axis=2)
    attended = attend(page_at, span_at, counts, queries, new_kv, positions, arrived)
    return attended, new_kv


def solution(mesh):
    split = Mesh(mesh.devices.reshape(4, 8, 4, 2), STORE + TENSOR)
    return jax.shard_map(
        body,
        mesh=split,
        in_specs=(
            P(STORE, TENSOR),
            P(TENSOR, STORE),
            P(STORE, None, TENSOR),
            P(STORE, TENSOR),
            P(),
            P(),
            P(STORE, None),
            P(STORE, None, None),
            P(STORE, None),
        ),
        out_specs=(P(STORE, TENSOR), P(STORE, TENSOR)),
        check_vma=False,
    )
```

```python
import functools

import jax
import jax.numpy as jnp
from jax import lax
from jax.experimental import pallas as pl
from jax.experimental.pallas import tpu as pltpu
from jax.sharding import Mesh
from jax.sharding import PartitionSpec as P

HEAD = 128
BF16 = jnp.bfloat16
F32 = jnp.float32
STORE = ("x", "z")
TENSOR = ("y", "core")
NEG = -1e30
EXP2_SCALE = 1.4426950408889634 * HEAD**-0.5


def pack_kernel(slot_ref, pages_ref, out_ref, sems):
    count = out_ref.shape[0]

    def copy(i):
        return pltpu.make_async_copy(pages_ref.at[slot_ref[i]], out_ref.at[i], sems.at[i])

    def start(i, carry):
        copy(i).start()
        return carry

    def wait(i, carry):
        copy(i).wait()
        return carry

    lax.fori_loop(0, count, start, 0)
    lax.fori_loop(0, count, wait, 0)


def pack_pages(source_slot, pages):
    count = source_slot.shape[0]
    return pl.pallas_call(
        pack_kernel,
        out_shape=jax.ShapeDtypeStruct((count,) + pages.shape[1:], pages.dtype),
        in_specs=[
            pl.BlockSpec(memory_space=pltpu.SMEM),
            pl.BlockSpec(memory_space=pl.ANY),
        ],
        out_specs=pl.BlockSpec(memory_space=pltpu.VMEM),
        scratch_shapes=[pltpu.SemaphoreType.DMA((count,))],
        cost_estimate=pl.CostEstimate(flops=0, bytes_accessed=1024, transcendentals=0),
    )(source_slot, pages)


def project_kernel(slot_ref, own_ref, other_ref, *rest):
    weights = rest[:4]
    outs = rest[4:8]
    held, sems = rest[8:]
    halves, slices, columns, width = weights[0].shape
    block = halves * columns
    copies = []
    for i in range(4):
        for j in range(halves):
            for s in range(slices):
                at = pl.multiple_of(slot_ref[i] * block + j * columns, columns)
                copies.append(
                    pltpu.make_async_copy(
                        weights[i].at[j, s], held.at[s, pl.ds(at, columns)], sems.at[i, j, s]
                    )
                )
    for copy in copies:
        copy.start()
    for copy in copies:
        copy.wait()
    step = 256
    for row in range(0, own_ref.shape[0], step):
        rows = slice(row, row + step)
        product = sum(
            lax.dot_general(
                ref[rows, :], held[s], (((1,), (1,)), ((), ())), preferred_element_type=F32
            )
            for s, ref in enumerate((own_ref, other_ref))
        )
        for i in range(4):
            outs[i][rows, :] = product[:, i * block : (i + 1) * block].astype(BF16)


def project(slots, own, other, weights):
    rows, width = own.shape
    halves, slices, columns, _ = weights[0].shape
    block = halves * columns
    vmem = pl.BlockSpec(memory_space=pltpu.VMEM)
    in_specs = [pl.BlockSpec(memory_space=pltpu.SMEM), vmem, vmem]
    in_specs += [pl.BlockSpec(memory_space=pl.ANY)] * 4
    return pl.pallas_call(
        project_kernel,
        out_shape=[jax.ShapeDtypeStruct((rows, block), BF16)] * 4,
        in_specs=in_specs,
        out_specs=[vmem] * 4,
        scratch_shapes=[
            pltpu.VMEM((slices, 4 * block, width), BF16),
            pltpu.SemaphoreType.DMA((4, halves, slices)),
        ],
        compiler_params=pltpu.CompilerParams(vmem_limit_bytes=40 << 20),
        cost_estimate=pl.CostEstimate(flops=0, bytes_accessed=1024, transcendentals=0),
    )(slots, own, other, *weights)


def attend_kernel(
    spans,
    per_span,
    page_ref,
    span_ref,
    count_ref,
    q_ref,
    new_ref,
    pos_row_ref,
    pos_lane_ref,
    arrived_ref,
    token_ref,
    out_ref,
    raw,
    keys,
    values,
    scores,
    weights,
    sems,
):
    requests = raw.shape[0]
    span_len = arrived_ref.shape[1]
    heads = q_ref.shape[1] // HEAD
    half = heads * per_span
    rows_request = spans * per_span

    def copy(r, k):
        return pltpu.make_async_copy(
            arrived_ref.at[page_ref[r, k]],
            raw.at[r, pl.ds(k * span_len, span_len)],
            sems.at[r, k],
        )

    for r in range(requests):
        for k in range(spans):
            copy(r, k).start()
    values[:, :, HEAD:] = jnp.ones((requests, spans * span_len, HEAD), BF16)
    place = lax.broadcasted_iota(jnp.int32, (span_len, per_span), 0)
    slot = lax.broadcasted_iota(jnp.int32, (span_len, per_span), 1)
    lane = lax.broadcasted_iota(jnp.int32, (per_span, span_len), 1)
    sub = lax.broadcasted_iota(jnp.int32, (per_span, HEAD), 0)
    groups = [(r, g) for r in range(requests) for g in range(spans // 2)]

    def blend(r, k):
        c = span_ref[r, k]
        pos = pos_row_ref[pl.ds(r * spans + c, 1), :]
        marked = (place == pos) & (slot < count_ref[r, c])
        first = pl.multiple_of(r * rows_request + c * per_span, per_span)
        fresh = new_ref[pl.ds(first, per_span), :]
        placed = jnp.dot(marked.astype(F32).astype(BF16), fresh, preferred_element_type=F32)
        replaced = jnp.max(marked.astype(F32), axis=1, keepdims=True) > 0.5
        at = slice(k * span_len, (k + 1) * span_len)
        mixed = jnp.where(replaced, placed, raw[r, at, :].astype(F32)).astype(BF16)
        keys[r, at, :] = mixed[:, :HEAD]
        values[r, at, :HEAD] = mixed[:, HEAD:]

    def first_row(r, k):
        return pl.multiple_of(r * rows_request + span_ref[r, k] * per_span, per_span)

    def score(step):
        r, g = groups[step]
        length = (g + 1) * 2 * span_len
        stacked = []
        for k in (2 * g, 2 * g + 1):
            block = q_ref[pl.ds(first_row(r, k), per_span), :]
            stacked += [block[:, h * HEAD : (h + 1) * HEAD] for h in range(heads)]
        scores[step % 2, :, :length] = lax.dot_general(
            jnp.concatenate(stacked, axis=0),
            keys[r, :length, :],
            (((1,), (1,)), ((), ())),
            preferred_element_type=F32,
        )

    def attend(step):
        r, g = groups[step]
        slot_now = step % 2
        length = (g + 1) * 2 * span_len
        for part, k in enumerate((2 * g, 2 * g + 1)):
            rows = slice(part * half, (part + 1) * half)
            own = k * span_len
            allowed = lane <= pos_lane_ref[pl.ds(first_row(r, k), per_span), :]
            allowed = jnp.concatenate([allowed] * heads, axis=0)
            diagonal = jnp.where(allowed, scores[slot_now, rows, own : own + span_len], NEG)
            peak = jnp.max(diagonal, axis=1, keepdims=True)
            if k:
                before = scores[slot_now, rows, :own]
                peak = jnp.maximum(peak, jnp.max(before, axis=1, keepdims=True))
                weights[slot_now, rows, :own] = jnp.exp2((before - peak) * EXP2_SCALE).astype(BF16)
            weights[slot_now, rows, own : own + span_len] = jnp.exp2(
                (diagonal - peak) * EXP2_SCALE
            ).astype(BF16)
            if own + span_len < length:
                weights[slot_now, rows, own + span_len : length] = jnp.zeros(
                    (half, length - own - span_len), BF16
                )
        mixed = jnp.dot(
            weights[slot_now, :, :length], values[r, :length, :], preferred_element_type=F32
        )
        mixed = mixed[:, :HEAD] / mixed[:, HEAD:]
        for part, k in enumerate((2 * g, 2 * g + 1)):
            used = sub < count_ref[r, span_ref[r, k]]
            for h in range(heads):
                at = part * half + h * per_span
                out_ref[pl.ds(first_row(r, k), per_span), h * HEAD : (h + 1) * HEAD] = jnp.where(
                    used, mixed[at : at + per_span], 0.0
                ).astype(BF16)

    for r in range(requests):
        for k in range(spans):
            copy(r, k).wait()
    for r in range(requests):
        for k in range(spans):
            blend(r, k)
    score(0)
    for step in range(len(groups)):
        if step + 1 < len(groups):
            score(step + 1)
        attend(step)


def attend(page_at, span_at, counts, queries, new_kv, positions, arrived, token):
    requests, spans = span_at.shape
    per_span = positions.shape[2]
    span_len = arrived.shape[1]
    kv_width = arrived.shape[2]
    heads = queries.shape[1] // HEAD
    length = spans * span_len
    pos_row = positions.reshape(requests * spans, per_span)
    pos_lane = jnp.broadcast_to(
        positions.reshape(requests * spans * per_span, 1), (requests * spans * per_span, span_len)
    )
    smem = pl.BlockSpec(memory_space=pltpu.SMEM)
    vmem = pl.BlockSpec(memory_space=pltpu.VMEM)
    pair = 2 * heads * per_span
    return pl.pallas_call(
        functools.partial(attend_kernel, spans, per_span),
        out_shape=jax.ShapeDtypeStruct(queries.shape, BF16),
        in_specs=[smem] * 3 + [vmem] * 4 + [pl.BlockSpec(memory_space=pl.ANY)] * 2,
        out_specs=vmem,
        scratch_shapes=[
            pltpu.VMEM((requests, length, kv_width), BF16),
            pltpu.VMEM((requests, length, HEAD), BF16),
            pltpu.VMEM((requests, length, 2 * HEAD), BF16),
            pltpu.VMEM((2, pair, length), F32),
            pltpu.VMEM((2, pair, length), BF16),
            pltpu.SemaphoreType.DMA((requests, spans)),
        ],
        compiler_params=pltpu.CompilerParams(vmem_limit_bytes=48 << 20),
        cost_estimate=pl.CostEstimate(flops=0, bytes_accessed=1024, transcendentals=0),
    )(page_at, span_at, counts, queries, new_kv, pos_row, pos_lane, arrived, token)


def shift(x, axis, by):
    size = lax.axis_size(axis)
    return lax.ppermute(x, axis, [(i, (i + by) % size) for i in range(size)])


def gather_over_z(pair):
    z = lax.axis_index("z")
    core = lax.axis_index("core")
    gathered = jnp.zeros((4,) + pair.shape, BF16)
    for by in range(4):
        near = []
        for hop in (by, by + 4):
            moves = [(s * 2 + s // 4, (s + hop) % 8 * 2 + s // 4) for s in range(8)]
            near.append(lax.ppermute(pair, ("z", "core"), moves) if hop else pair)
        first = (z - by) % 8 // 4 == core
        piece = jnp.where(first, near[0], near[1])
        gathered = lax.dynamic_update_slice(gathered, piece[None], ((z - by) % 4, 0, 0, 0))
    return gathered


def new_rows(hidden, other, gathered):
    ahead = (lax.axis_index("x") - lax.axis_index("y") - jnp.arange(4)) % 4
    keys, values = gathered[:2], gathered[2:]
    keys_left, values_right = shift(keys, "x", 1), shift(values, "x", 3)
    values_left, keys_right = shift(values, "x", 1), shift(keys, "x", 3)
    keys_far, values_far = shift(keys_left, "x", 1), shift(values_right, "x", 3)
    parts = [
        [keys, keys_left, keys_far, keys_right],
        [values, values_left, values_far, values_right],
    ]
    totals = []
    for weights in parts:
        if totals:
            weights[0], products = lax.optimization_barrier((weights[0], products))
            received = [shift(products[by], "y", by) for by in (1, 3, 2)]
            totals[0] = sum((p.astype(F32) for p in received), products[0].astype(F32))
        products = project(ahead, hidden, other, weights)
        if not totals:
            totals.append(None)
        else:
            received = [shift(products[by], "y", by) for by in (1, 3, 2)]
            totals.append(sum((p.astype(F32) for p in received), products[0].astype(F32)))
    return jnp.concatenate(totals, axis=1)


def body(hidden, kv_weight, pages, queries, page_owner, page_slot, span_order, positions, counts):
    stores = lax.axis_size(STORE)
    tensors = lax.axis_size(TENSOR)
    store_index = lax.axis_index(STORE)
    requests, spans = span_order.shape
    per_span = positions.shape[2]
    entries = requests * spans
    span_len, kv_width = pages.shape[1:]

    owners = page_owner.reshape(stores, entries)
    slots = page_slot.reshape(stores, entries)
    entry = jnp.arange(entries)[None, :]
    mine = owners == store_index
    code = entry * pages.shape[0] + slots
    first = jnp.min(jnp.where(mine, code, entries * pages.shape[0]), axis=1)
    last = jnp.max(jnp.where(mine, code, 0), axis=1)
    source_slot = jnp.stack([first, last], axis=1).reshape(-1) % pages.shape[0]
    outgoing = pack_pages(source_slot, pages)
    shard, outgoing = lax.optimization_barrier((kv_weight.T, outgoing))
    pair = jnp.stack([shard, shift(shard, "core", 1)])
    gathered = gather_over_z(pair)
    other = shift(hidden, "core", 1)
    gathered, other = lax.optimization_barrier((gathered, other))
    outgoing = outgoing.reshape(4, 8, 2, span_len, kv_width)
    halfway = lax.all_to_all(outgoing, "x", split_axis=0, concat_axis=0, tiled=True)
    halfway = halfway.transpose(1, 0, 2, 3, 4)
    halfway, token = lax.optimization_barrier((halfway, gathered))
    arrived = lax.all_to_all(halfway, "z", split_axis=0, concat_axis=0, tiled=True)
    arrived = arrived.reshape(stores * 2, span_len, kv_width)

    own_kv = new_rows(hidden, other, gathered)
    row_used = jnp.arange(per_span)[None, None, :] < counts[:, :, None]
    new_kv = jnp.where(row_used.reshape(-1, 1), own_kv, 0.0).astype(BF16)

    my_owner = lax.dynamic_index_in_dim(owners, store_index, 0, keepdims=False)
    earlier = jnp.arange(entries)[None, :] < jnp.arange(entries)[:, None]
    second = jnp.any((my_owner[:, None] == my_owner[None, :]) & earlier, axis=1)
    page_of = ((my_owner % 8 * 4 + my_owner // 8) * 2 + second.astype(jnp.int32)).reshape(requests, spans)
    at_rank = span_order[:, None, :] == jnp.arange(spans)[None, :, None]
    span_at = jnp.sum(at_rank * jnp.arange(spans)[None, None, :], axis=2)
    page_at = jnp.sum(at_rank * page_of[:, None, :], axis=2)
    attended = attend(page_at, span_at, counts, queries, new_kv, positions, arrived, token)
    return attended, new_kv


def solution(mesh):
    split = Mesh(mesh.devices.reshape(4, 8, 4, 2), STORE + TENSOR)
    return jax.shard_map(
        body,
        mesh=split,
        in_specs=(
            P(STORE, TENSOR),
            P(TENSOR, STORE),
            P(STORE, None, TENSOR),
            P(STORE, TENSOR),
            P(),
            P(),
            P(STORE, None),
            P(STORE, None, None),
            P(STORE, None),
        ),
        out_specs=(P(STORE, TENSOR), P(STORE, TENSOR)),
        check_vma=False,
    )
```

```python
import functools

import jax
import jax.numpy as jnp
from jax import lax
from jax.experimental import pallas as pl
from jax.experimental.pallas import tpu as pltpu
from jax.sharding import Mesh
from jax.sharding import PartitionSpec as P

HEAD = 128
BF16 = jnp.bfloat16
F32 = jnp.float32
STORE = ("x", "z")
TENSOR = ("y", "core")
NEG = -1e30
EXP2_SCALE = 1.4426950408889634 * HEAD**-0.5


def pack_kernel(slot_ref, pages_ref, out_ref, sems):
    count = out_ref.shape[0]

    def copy(i):
        return pltpu.make_async_copy(pages_ref.at[slot_ref[i]], out_ref.at[i], sems.at[i])

    def start(i, carry):
        copy(i).start()
        return carry

    def wait(i, carry):
        copy(i).wait()
        return carry

    lax.fori_loop(0, count, start, 0)
    lax.fori_loop(0, count, wait, 0)


def pack_pages(source_slot, pages):
    count = source_slot.shape[0]
    return pl.pallas_call(
        pack_kernel,
        out_shape=jax.ShapeDtypeStruct((count,) + pages.shape[1:], pages.dtype),
        in_specs=[
            pl.BlockSpec(memory_space=pltpu.SMEM),
            pl.BlockSpec(memory_space=pl.ANY),
        ],
        out_specs=pl.BlockSpec(memory_space=pltpu.VMEM),
        scratch_shapes=[pltpu.SemaphoreType.DMA((count,))],
        cost_estimate=pl.CostEstimate(flops=0, bytes_accessed=1024, transcendentals=0),
    )(source_slot, pages)


def project_kernel(slot_ref, own_ref, other_ref, *rest):
    weights = rest[:4]
    outs = rest[4:8]
    held, sems = rest[8:]
    halves, slices, columns, width = weights[0].shape
    block = halves * columns
    copies = []
    for i in range(4):
        for j in range(halves):
            for s in range(slices):
                at = pl.multiple_of(slot_ref[i] * block + j * columns, columns)
                copies.append(
                    pltpu.make_async_copy(
                        weights[i].at[j, s], held.at[s, pl.ds(at, columns)], sems.at[i, j, s]
                    )
                )
    for copy in copies:
        copy.start()
    for copy in copies:
        copy.wait()
    step = 256
    for row in range(0, own_ref.shape[0], step):
        rows = slice(row, row + step)
        product = sum(
            lax.dot_general(
                ref[rows, :], held[s], (((1,), (1,)), ((), ())), preferred_element_type=F32
            )
            for s, ref in enumerate((own_ref, other_ref))
        )
        for i in range(4):
            outs[i][rows, :] = product[:, i * block : (i + 1) * block].astype(BF16)


def project(slots, own, other, weights):
    rows, width = own.shape
    halves, slices, columns, _ = weights[0].shape
    block = halves * columns
    vmem = pl.BlockSpec(memory_space=pltpu.VMEM)
    in_specs = [pl.BlockSpec(memory_space=pltpu.SMEM), vmem, vmem]
    in_specs += [pl.BlockSpec(memory_space=pl.ANY)] * 4
    return pl.pallas_call(
        project_kernel,
        out_shape=[jax.ShapeDtypeStruct((rows, block), BF16)] * 4,
        in_specs=in_specs,
        out_specs=[vmem] * 4,
        scratch_shapes=[
            pltpu.VMEM((slices, 4 * block, width), BF16),
            pltpu.SemaphoreType.DMA((4, halves, slices)),
        ],
        compiler_params=pltpu.CompilerParams(vmem_limit_bytes=40 << 20),
        cost_estimate=pl.CostEstimate(flops=0, bytes_accessed=1024, transcendentals=0),
    )(slots, own, other, *weights)


def attend_kernel(
    spans,
    per_span,
    page_ref,
    span_ref,
    count_ref,
    q_ref,
    new_ref,
    pos_row_ref,
    pos_lane_ref,
    arrived_ref,
    token_ref,
    out_ref,
    raw,
    keys,
    values,
    scores,
    weights,
    sems,
):
    requests = raw.shape[0]
    span_len = arrived_ref.shape[1]
    heads = q_ref.shape[1] // HEAD
    half = heads * per_span
    rows_request = spans * per_span

    def copy(r, k):
        return pltpu.make_async_copy(
            arrived_ref.at[page_ref[r, k]],
            raw.at[r, pl.ds(k * span_len, span_len)],
            sems.at[r, k],
        )

    for r in range(requests):
        for k in range(spans):
            copy(r, k).start()
    values[:, :, HEAD:] = jnp.ones((requests, spans * span_len, HEAD), BF16)
    place = lax.broadcasted_iota(jnp.int32, (span_len, per_span), 0)
    slot = lax.broadcasted_iota(jnp.int32, (span_len, per_span), 1)
    lane = lax.broadcasted_iota(jnp.int32, (per_span, span_len), 1)
    sub = lax.broadcasted_iota(jnp.int32, (per_span, HEAD), 0)
    groups = [(r, g) for r in range(requests) for g in range(spans // 2)]

    def blend(r, k):
        c = span_ref[r, k]
        pos = pos_row_ref[pl.ds(r * spans + c, 1), :]
        marked = (place == pos) & (slot < count_ref[r, c])
        first = pl.multiple_of(r * rows_request + c * per_span, per_span)
        fresh = new_ref[pl.ds(first, per_span), :]
        placed = jnp.dot(marked.astype(F32).astype(BF16), fresh, preferred_element_type=F32)
        replaced = jnp.max(marked.astype(F32), axis=1, keepdims=True) > 0.5
        at = slice(k * span_len, (k + 1) * span_len)
        mixed = jnp.where(replaced, placed, raw[r, at, :].astype(F32)).astype(BF16)
        keys[r, at, :] = mixed[:, :HEAD]
        values[r, at, :HEAD] = mixed[:, HEAD:]

    def first_row(r, k):
        return pl.multiple_of(r * rows_request + span_ref[r, k] * per_span, per_span)

    def score(step):
        r, g = groups[step]
        length = (g + 1) * 2 * span_len
        stacked = []
        for k in (2 * g, 2 * g + 1):
            block = q_ref[pl.ds(first_row(r, k), per_span), :]
            stacked += [block[:, h * HEAD : (h + 1) * HEAD] for h in range(heads)]
        scores[step % 2, :, :length] = lax.dot_general(
            jnp.concatenate(stacked, axis=0),
            keys[r, :length, :],
            (((1,), (1,)), ((), ())),
            preferred_element_type=F32,
        )

    def attend(step):
        r, g = groups[step]
        slot_now = step % 2
        length = (g + 1) * 2 * span_len
        for part, k in enumerate((2 * g, 2 * g + 1)):
            rows = slice(part * half, (part + 1) * half)
            own = k * span_len
            allowed = lane <= pos_lane_ref[pl.ds(first_row(r, k), per_span), :]
            allowed = jnp.concatenate([allowed] * heads, axis=0)
            diagonal = jnp.where(allowed, scores[slot_now, rows, own : own + span_len], NEG)
            peak = jnp.max(diagonal, axis=1, keepdims=True)
            if k:
                before = scores[slot_now, rows, :own]
                peak = jnp.maximum(peak, jnp.max(before, axis=1, keepdims=True))
                weights[slot_now, rows, :own] = jnp.exp2((before - peak) * EXP2_SCALE).astype(BF16)
            weights[slot_now, rows, own : own + span_len] = jnp.exp2(
                (diagonal - peak) * EXP2_SCALE
            ).astype(BF16)
            if own + span_len < length:
                weights[slot_now, rows, own + span_len : length] = jnp.zeros(
                    (half, length - own - span_len), BF16
                )
        mixed = jnp.dot(
            weights[slot_now, :, :length], values[r, :length, :], preferred_element_type=F32
        )
        mixed = mixed[:, :HEAD] / mixed[:, HEAD:]
        for part, k in enumerate((2 * g, 2 * g + 1)):
            used = sub < count_ref[r, span_ref[r, k]]
            for h in range(heads):
                at = part * half + h * per_span
                out_ref[pl.ds(first_row(r, k), per_span), h * HEAD : (h + 1) * HEAD] = jnp.where(
                    used, mixed[at : at + per_span], 0.0
                ).astype(BF16)

    for r in range(requests):
        for k in range(spans):
            copy(r, k).wait()
    for r in range(requests):
        for k in range(spans):
            blend(r, k)
    score(0)
    for step in range(len(groups)):
        if step + 1 < len(groups):
            score(step + 1)
        attend(step)


def attend(page_at, span_at, counts, queries, new_kv, positions, arrived, token):
    requests, spans = span_at.shape
    per_span = positions.shape[2]
    span_len = arrived.shape[1]
    kv_width = arrived.shape[2]
    heads = queries.shape[1] // HEAD
    length = spans * span_len
    pos_row = positions.reshape(requests * spans, per_span)
    pos_lane = jnp.broadcast_to(
        positions.reshape(requests * spans * per_span, 1), (requests * spans * per_span, span_len)
    )
    smem = pl.BlockSpec(memory_space=pltpu.SMEM)
    vmem = pl.BlockSpec(memory_space=pltpu.VMEM)
    pair = 2 * heads * per_span
    return pl.pallas_call(
        functools.partial(attend_kernel, spans, per_span),
        out_shape=jax.ShapeDtypeStruct(queries.shape, BF16),
        in_specs=[smem] * 3 + [vmem] * 4 + [pl.BlockSpec(memory_space=pl.ANY)] * 2,
        out_specs=vmem,
        scratch_shapes=[
            pltpu.VMEM((requests, length, kv_width), BF16),
            pltpu.VMEM((requests, length, HEAD), BF16),
            pltpu.VMEM((requests, length, 2 * HEAD), BF16),
            pltpu.VMEM((2, pair, length), F32),
            pltpu.VMEM((2, pair, length), BF16),
            pltpu.SemaphoreType.DMA((requests, spans)),
        ],
        compiler_params=pltpu.CompilerParams(vmem_limit_bytes=48 << 20),
        cost_estimate=pl.CostEstimate(flops=0, bytes_accessed=1024, transcendentals=0),
    )(page_at, span_at, counts, queries, new_kv, pos_row, pos_lane, arrived, token)


def shift(x, axis, by):
    size = lax.axis_size(axis)
    return lax.ppermute(x, axis, [(i, (i + by) % size) for i in range(size)])


def gather_over_z(pair):
    z = lax.axis_index("z")
    core = lax.axis_index("core")
    gathered = jnp.zeros((4,) + pair.shape, BF16)
    for by in range(4):
        near = []
        for hop in (by, by + 4):
            moves = [(s * 2 + s // 4, (s + hop) % 8 * 2 + s // 4) for s in range(8)]
            near.append(lax.ppermute(pair, ("z", "core"), moves) if hop else pair)
        first = (z - by) % 8 // 4 == core
        piece = jnp.where(first, near[0], near[1])
        gathered = lax.dynamic_update_slice(gathered, piece[None], ((z - by) % 4, 0, 0, 0))
    return gathered


def new_rows(hidden, other, gathered):
    ahead = (lax.axis_index("x") - lax.axis_index("y") - jnp.arange(4)) % 4
    keys, values = gathered[:2], gathered[2:]
    keys_left, values_right = shift(keys, "x", 1), shift(values, "x", 3)
    values_left, keys_right = shift(values, "x", 1), shift(keys, "x", 3)
    keys_far, values_far = shift(keys_left, "x", 1), shift(values_right, "x", 3)
    parts = [
        [keys, keys_left, keys_far, keys_right],
        [values, values_left, values_far, values_right],
    ]
    totals = []
    for weights in parts:
        if totals:
            weights[0], products = lax.optimization_barrier((weights[0], products))
            received = [shift(products[by], "y", by) for by in (1, 3, 2)]
            totals[0] = sum((p.astype(F32) for p in received), products[0].astype(F32))
        products = project(ahead, hidden, other, weights)
        if not totals:
            totals.append(None)
        else:
            received = [shift(products[by], "y", by) for by in (1, 3, 2)]
            totals.append(sum((p.astype(F32) for p in received), products[0].astype(F32)))
    return jnp.concatenate(totals, axis=1)


def body(hidden, kv_weight, pages, queries, page_owner, page_slot, span_order, positions, counts):
    stores = lax.axis_size(STORE)
    tensors = lax.axis_size(TENSOR)
    store_index = lax.axis_index(STORE)
    requests, spans = span_order.shape
    per_span = positions.shape[2]
    entries = requests * spans
    span_len, kv_width = pages.shape[1:]

    depth = pages.shape[0]
    row = jnp.arange(page_owner.shape[0])[:, None] % requests
    mine = page_owner == store_index
    code = (row * spans + jnp.arange(spans)[None, :]) * depth + page_slot
    first = jnp.min(jnp.where(mine, code, entries * depth), axis=1)
    last = jnp.max(jnp.where(mine, code, 0), axis=1)
    first = jnp.min(first.reshape(stores, requests), axis=1)
    last = jnp.max(last.reshape(stores, requests), axis=1)
    source_slot = jnp.stack([first, last], axis=1).reshape(-1) % depth
    outgoing = pack_pages(source_slot, pages)
    shard, outgoing = lax.optimization_barrier((kv_weight.T, outgoing))
    pair = jnp.stack([shard, shift(shard, "core", 1)])
    gathered = gather_over_z(pair)
    other = shift(hidden, "core", 1)
    gathered, other = lax.optimization_barrier((gathered, other))
    outgoing = outgoing.reshape(4, 8, 2, span_len, kv_width)
    halfway = lax.all_to_all(outgoing, "x", split_axis=0, concat_axis=0, tiled=True)
    halfway = halfway.transpose(1, 0, 2, 3, 4)
    halfway, token = lax.optimization_barrier((halfway, gathered))
    arrived = lax.all_to_all(halfway, "z", split_axis=0, concat_axis=0, tiled=True)
    arrived = arrived.reshape(stores * 2, span_len, kv_width)

    own_kv = new_rows(hidden, other, gathered)
    row_used = jnp.arange(per_span)[None, None, :] < counts[:, :, None]
    new_kv = jnp.where(row_used.reshape(-1, 1), own_kv, 0.0).astype(BF16)

    my_owner = lax.dynamic_slice_in_dim(page_owner, store_index * requests, requests, 0)
    my_owner = my_owner.reshape(entries)
    earlier = jnp.arange(entries)[None, :] < jnp.arange(entries)[:, None]
    second = jnp.any((my_owner[:, None] == my_owner[None, :]) & earlier, axis=1)
    page_of = ((my_owner % 8 * 4 + my_owner // 8) * 2 + second.astype(jnp.int32)).reshape(requests, spans)
    at_rank = span_order[:, None, :] == jnp.arange(spans)[None, :, None]
    span_at = jnp.sum(at_rank * jnp.arange(spans)[None, None, :], axis=2)
    page_at = jnp.sum(at_rank * page_of[:, None, :], axis=2)
    attended = attend(page_at, span_at, counts, queries, new_kv, positions, arrived, token[0, 0, :16, :HEAD])
    return attended, new_kv


def solution(mesh):
    split = Mesh(mesh.devices.reshape(4, 8, 4, 2), STORE + TENSOR)
    return jax.shard_map(
        body,
        mesh=split,
        in_specs=(
            P(STORE, TENSOR),
            P(TENSOR, STORE),
            P(STORE, None, TENSOR),
            P(STORE, TENSOR),
            P(),
            P(),
            P(STORE, None),
            P(STORE, None, None),
            P(STORE, None),
        ),
        out_specs=(P(STORE, TENSOR), P(STORE, TENSOR)),
        check_vma=False,
    )
```
